256 devices in a mesh: pairs: 64 (over y, z, core), dom: 4 (over x).
Axes of the slice: x: 4, y: 4, z: 8, core: 2. Of those that a mesh axis runs over, the one named last changes fastest.
Arguments:
- amplitude: bfloat16 [512, 384, 384], P('pairs', 'dom'), may hold values from -2 to 2
- integrals: bfloat16 [512, 384, 384], P('pairs', 'dom'), may hold values from -6 to 6
- virtual_energy: float32 [512, 384], P('pairs'), may hold values from 0.2 to 1.5
- occupied_gap: float32 [512], P('pairs'), may hold values from 0.3 to 1.5
- pair_slot: int32 [512], replicated, may hold values from 0 to 511, as said below
- coupling_source: int32 [8192], replicated, may hold values from 0 to 511, as said below
- coupling_target: int32 [8192], replicated, may hold values from 0 to 511, as said below
- coupling_fock: float32 [8192], P(('pairs', 'dom')), may hold values from -3 to 3
- coupling_intersection: bfloat16 [8192, 384, 384], P(('pairs', 'dom')), may hold values from -0.3125 to 0.3125
Outputs:
- updated_amplitude: float32 [512, 384, 384], P('pairs', 'dom')
- residual: float32 [512, 384, 384], P('pairs', 'dom')
The draws below stay inside these ranges and needn't reach their ends.
Inputs may be any that keep to these rules, and one draw needn't show every extreme that they name: A permutation: pair p is stored at position pair_slot[p], which lies on index pair_slot[p] // 8 of pairs. `coupling_target`: coupling c is held by index c // 128 of pairs, and its target pair is stored on that same index; the two couplings that share a source pair on one holder have different targets. `coupling_source`: among the 128 couplings of one holder, every source pair appears in exactly two, and there are 64 distinct source pairs; of the pairs stored on any one index of pairs, a holder uses at most 2 distinct ones as sources, and exactly 2 for some indices on every holder.
All inputs are finite; a program needn't handle non-finite values.
Results may differ from the reference program's by a relative error of at most 0.0024.
Values may be sent and summed in bfloat16 or wider, within the bound.
No kernel may reach another device: no remote copies, remote signals or barrier semaphores. Data moves between devices by JAX's collectives and lax.ppermute only.
A program may use at most 128 MiB of HBM per device.

```python
import math
import jax
import jax.numpy as jnp
from jax import lax

W = 384
PAIR_DEV = 8
UPDATES = 1
PAIRS = 512
CPL_DEV = 128
COUPLINGS = 8192
N_DOM = 4


def shuffle_rows(keys, length):

    def one_row(row_key):
        return jax.random.permutation(row_key, length)
    return jax.vmap(one_row)(keys).astype(jnp.int32)


def coupling_tables(key):
    base = jax.random.fold_in(key, 7101)
    keys = jax.random.split(base, 8)
    holders = PAIRS // PAIR_DEV
    doubled = 3 * holders // 8
    single = holders // 4
    pair_slot = jax.random.permutation(keys[0], PAIRS).astype(jnp.int32)
    slot_pair = jnp.argsort(pair_slot).astype(jnp.int32)
    owner_order = shuffle_rows(jax.random.split(keys[1], holders), holders)
    twice = owner_order[:, :doubled]
    once = owner_order[:, doubled:doubled + single]
    first_local = jax.random.randint(keys[2], (holders, doubled), 0, PAIR_DEV)
    second_local = (first_local + 1 + jax.random.randint(keys[3], (holders, doubled), 0, PAIR_DEV - 1)) % PAIR_DEV
    once_local = jax.random.randint(keys[4], (holders, single), 0, PAIR_DEV)
    owners = jnp.concatenate([twice, twice, once], axis=1)
    local_index = jnp.concatenate([first_local, second_local, once_local], axis=1)
    sources = owners * PAIR_DEV + local_index
    first_target = jax.random.randint(keys[5], sources.shape, 0, PAIR_DEV)
    second_target = (first_target + 1 + jax.random.randint(keys[6], sources.shape, 0, PAIR_DEV - 1)) % PAIR_DEV
    holder_base = jnp.arange(holders, dtype=jnp.int32)[:, None] * PAIR_DEV
    source_all = jnp.concatenate([sources, sources], axis=1)
    target_all = jnp.concatenate([first_target, second_target], axis=1) + holder_base
    shuffle = shuffle_rows(jax.random.split(keys[7], holders), CPL_DEV)
    source_all = jnp.take_along_axis(source_all, shuffle, axis=1).reshape(-1)
    target_all = jnp.take_along_axis(target_all, shuffle, axis=1).reshape(-1)
    return (pair_slot, jnp.take(slot_pair, source_all).astype(jnp.int32), jnp.take(slot_pair, target_all).astype(jnp.int32))


def draw_pair_slot(key, part):
    return coupling_tables(key)[0]


def draw_coupling_source(key, part):
    return coupling_tables(key)[1]


def draw_coupling_target(key, part):
    return coupling_tables(key)[2]


def steps_of(key, shape, shards, low, high):
    level = 1.0
    for position, shards_of in shards:
        draws = jax.random.uniform(jax.random.fold_in(jax.random.fold_in(key, 6), position), (shards_of,), jnp.float32, low / len(shards), high / len(shards))
        level = level * jnp.repeat(jnp.exp(draws), shape[position] // shards_of).reshape((-1,) + (1,) * (len(shape) - 1 - position))
    return level


def gaussian(stream_key, dims, spread, most, shards=(), kind=jnp.bfloat16):
    entries = spread * jax.random.normal(stream_key, dims, jnp.float32)
    if shards:
        entries = entries * steps_of(stream_key, dims, shards, -0.22, 0.18)
    return jnp.clip(entries, -most, most).astype(kind)


def setup_inputs(seed: int = 0) -> dict:
    key_of = jax.random.split(jax.random.key(seed), 10)
    return {
        "amplitude": gaussian(key_of[0], (PAIRS, W, W), 0.3, 2.0, ((0, 64), (1, 4))),
        "integrals": gaussian(key_of[1], (PAIRS, W, W), 1.0, 6.0, ((0, 64), (1, 4))),
        "virtual_energy": jnp.clip(jnp.exp(math.log(1.5) - 2.014903 * jax.random.uniform(key_of[2], (PAIRS, W), jnp.float32) ** steps_of(key_of[2], (PAIRS, W), ((0, 64),), -0.2, 0.2)), 0.2, 1.5),
        "occupied_gap": jnp.clip(jnp.exp(math.log(1.5) - 1.60943787 * jax.random.uniform(key_of[3], (PAIRS,), jnp.float32) ** steps_of(key_of[3], (PAIRS,), ((0, 64),), -0.2, 0.2)), 0.3, 1.5),
        "pair_slot": draw_pair_slot(jax.random.fold_in(key_of[9], 71), 0),
        "coupling_source": draw_coupling_source(jax.random.fold_in(key_of[9], 71), 0),
        "coupling_target": draw_coupling_target(jax.random.fold_in(key_of[9], 71), 0),
        "coupling_fock": gaussian(key_of[7], (COUPLINGS,), 0.5, 3.0, ((0, 256),), jnp.float32),
        "coupling_intersection": gaussian(key_of[8], (COUPLINGS, W, W), W ** -0.5, 0.3125, ((0, 256),)),
    }


def reference(amplitude, integrals, virtual_energy, occupied_gap, pair_slot, coupling_source, coupling_target, coupling_fock, coupling_intersection):
    source_slot = jnp.take(pair_slot, coupling_source).astype(jnp.int32)
    target_slot = jnp.take(pair_slot, coupling_target).astype(jnp.int32)
    denominator = virtual_energy[:, :, None] + virtual_energy[:, None, :] + occupied_gap[:, None, None]
    current = amplitude.astype(jnp.float32)
    block = CPL_DEV // N_DOM
    blocks = COUPLINGS // block
    residual = jnp.zeros(current.shape, jnp.float32)
    for step in range(UPDATES):
        sent = current.astype(jnp.bfloat16)

        def add_block(total, index):
            start = (index * block).astype(jnp.int32)
            sources = lax.dynamic_slice_in_dim(source_slot, start, block)
            targets = lax.dynamic_slice_in_dim(target_slot, start, block)
            fock = lax.dynamic_slice_in_dim(coupling_fock, start, block)
            intersection = lax.dynamic_slice_in_dim(coupling_intersection, start, block).astype(jnp.float32)
            picked = jnp.take(sent, sources, axis=0).astype(jnp.float32)
            left = jnp.einsum("cab,cbd->cad", intersection, picked).astype(jnp.bfloat16)
            left = lax.optimization_barrier(left).astype(jnp.float32)
            projected = jnp.einsum("cad,ced->cae", left, intersection)
            coupled_term = (fock[:, None, None] * projected).astype(jnp.bfloat16)
            coupled_term = lax.optimization_barrier(coupled_term).astype(jnp.float32)
            return total.at[targets].add(coupled_term), None

        coupled, unused = lax.scan(add_block, jnp.zeros(current.shape, jnp.float32), jnp.arange(blocks, dtype=jnp.int32))
        residual = integrals.astype(jnp.float32) + denominator * current - coupled
        current = current - residual / denominator
    return current, residual
```

```python
import jax
import jax.numpy as jnp
from jax import lax
from jax.experimental import pallas as pl
from jax.experimental.pallas import tpu as pltpu
from jax.sharding import Mesh, PartitionSpec as P

COLUMNS = 128
SPLITS = 2
GROUPS = (
    ("ring", ((0, 0),)),
    ("gather", ((0, 1), (1, 0), (1, 1), (2, 0), (2, 1))),
)
STAGES = ((0, 1), (2,))
UNROLL = 4
RING_PLACE = (0, 2, 4, 6, 7, 5, 3, 1)
STAGE_FLOPS = 12_000_000_000
STAGE_BYTES = 36_000_000


def lookup(table, indices):
    places = jnp.arange(table.shape[0], dtype=jnp.int32)
    return jnp.sum(jnp.where(indices[..., None] == places, table, 0), axis=-1)


def ring_gather(block):
    count = lax.axis_size("z")
    up = [(i, (i + 1) % count) for i in range(count)]
    down = [(i, (i - 1) % count) for i in range(count)]
    parts = [block]
    above = below = block
    for _ in range(count // 2 - 1):
        above = lax.ppermute(above, "z", up)
        below = lax.ppermute(below, "z", down)
        parts += [above, below]
    half = block.shape[1] // 2
    above = lax.ppermute(above[:, :half], "z", up)
    below = lax.ppermute(below[:, half:], "z", down)
    parts.append(jnp.concatenate([above, below], axis=1))
    return jnp.stack(parts)


def split(amplitude, piece):
    pairs, _, _ = amplitude.shape

    def kernel(in_ref, *out_refs):
        for out_ref, (_, members) in zip(out_refs, GROUPS):
            for n, (j, r) in enumerate(members):
                rows = slice(r * piece, (r + 1) * piece)
                lanes = slice(j * COLUMNS, (j + 1) * COLUMNS)
                for p in range(pairs):
                    out_ref[n, p] = in_ref[p, rows, lanes]

    return pl.pallas_call(
        kernel,
        out_shape=[
            jax.ShapeDtypeStruct((len(members), pairs, piece, COLUMNS), amplitude.dtype)
            for _, members in GROUPS
        ],
        name="split",
    )(amplitude)


def pick(arrays, member, index, outputs, name, cost=None):
    piece, lanes = arrays[0].shape[-2:]
    count = index.shape[0] // outputs
    sizes = [array.shape[0] * array.shape[2] for array in arrays]

    def kernel(index_ref, *refs):
        in_refs = refs[: len(arrays)]
        out_refs = refs[len(arrays) : len(arrays) + outputs]
        held, sems = refs[-2:]
        copies = []
        start = 0
        for n, ref in enumerate(in_refs):
            for lead in range(arrays[n].shape[0]):
                size = arrays[n].shape[2]
                copy = pltpu.make_async_copy(
                    ref.at[lead, member], held.at[pl.ds(start, size)], sems.at[len(copies)]
                )
                copy.start()
                copies.append(copy)
                start += size
        for copy in copies:
            copy.wait()

        def body(i, carry):
            for n in range(outputs):
                out_refs[n][i] = held[index_ref[n * count + i]]
            return carry

        lax.fori_loop(0, count, body, 0, unroll=8)

    result = pl.pallas_call(
        kernel,
        in_specs=[pl.BlockSpec(memory_space=pltpu.SMEM)] + [pl.BlockSpec(memory_space=pltpu.HBM if array.shape[1] > 1 else pl.ANY) for array in arrays],
        out_specs=[pl.BlockSpec(memory_space=pltpu.VMEM)] * outputs,
        out_shape=[jax.ShapeDtypeStruct((count, piece, lanes), arrays[0].dtype)] * outputs,
        scratch_shapes=[
            pltpu.VMEM((sum(sizes), piece, lanes), arrays[0].dtype),
            pltpu.SemaphoreType.DMA((sum(array.shape[0] for array in arrays),)),
        ],
        compiler_params=pltpu.CompilerParams(vmem_limit_bytes=60 * 1024 * 1024),
        cost_estimate=cost,
        name=name,
    )(index, *arrays)
    return result


def make_couple(stage, first, final, count, rows, width, pairs, quarters):
    columns = len(stage) * COLUMNS
    begin = stage[0] * COLUMNS
    blocks = len(stage) * SPLITS
    piece = rows // SPLITS

    def kernel(target, fock, s_ref, *rest):
        rest = list(rest)
        amp_refs = [rest.pop(0) for _ in range(blocks)]
        base_ref = None if first else rest.pop(0)
        out_ref = rest.pop(0)
        acc = rest.pop(0) if final else out_ref
        step = pl.program_id(0)

        @pl.when(step == 0)
        def _():
            for p in range(pairs):
                if first:
                    acc[p] = jnp.zeros((width, width), jnp.float32)
                else:
                    acc[p] = base_ref[p]

        lefts = []
        for g in range(UNROLL):
            strips = []
            for b in range(0, blocks, SPLITS):
                pieces = [amp_refs[b + r][q, g] for q in range(quarters) for r in range(SPLITS)]
                strips.append(jnp.concatenate(pieces, axis=0))
            amp = strips[0] if len(strips) == 1 else jnp.concatenate(strips, axis=1)
            left = jnp.dot(s_ref[g], amp, preferred_element_type=jnp.float32)
            lefts.append(left.astype(jnp.bfloat16))
        for g in range(UNROLL):
            part = lax.dot_general(
                lefts[g],
                s_ref[g, :, begin : begin + columns],
                (((1,), (1,)), ((), ())),
                preferred_element_type=jnp.float32,
            )
            c = step * UNROLL + g
            acc[target[c]] += fock[c] * part
        if final:

            @pl.when(step == count // UNROLL - 1)
            def _():
                for p in range(pairs):
                    for q in range(quarters):
                        out_ref[q, p] = acc[p, q * rows : (q + 1) * rows, :].astype(jnp.bfloat16)

    whole = pl.BlockSpec((pairs, width, width), lambda i, *_: (0, 0, 0), pipeline_mode=pl.Buffered(1))
    in_specs = [pl.BlockSpec((UNROLL, width, width), lambda i, *_: (i, 0, 0))]
    in_specs += [pl.BlockSpec((quarters, UNROLL, piece, COLUMNS), lambda i, *_: (0, i, 0, 0))] * blocks
    if not first:
        in_specs.append(whole)
    scratch = []
    if final:
        out_shape = jax.ShapeDtypeStruct((quarters, pairs, rows, width), jnp.bfloat16)
        out_specs = pl.BlockSpec((quarters, pairs, rows, width), lambda i, *_: (0, 0, 0, 0))
        scratch.append(pltpu.VMEM((pairs, width, width), jnp.float32))
    else:
        out_shape = jax.ShapeDtypeStruct((pairs, width, width), jnp.float32)
        out_specs = whole
    return pl.pallas_call(
        kernel,
        grid_spec=pltpu.PrefetchScalarGridSpec(
            num_scalar_prefetch=2,
            grid=(count // UNROLL,),
            in_specs=in_specs,
            out_specs=out_specs,
            scratch_shapes=scratch,
        ),
        out_shape=out_shape,
        compiler_params=pltpu.CompilerParams(vmem_limit_bytes=60 * 1024 * 1024),
        cost_estimate=pl.CostEstimate(
            flops=8 * count * width * width * columns,
            bytes_accessed=count * width * width * 3,
            transcendentals=0,
        ),
        name="couple",
    )


def per_device(
    amplitude,
    integrals,
    virtual_energy,
    occupied_gap,
    pair_slot,
    coupling_source,
    coupling_target,
    coupling_fock,
    coupling_intersection,
):
    ny, nz, nc, quarters = (lax.axis_size(a) for a in ("y", "z", "core", "dom"))
    y, z, core, me = (lax.axis_index(a) for a in ("y", "z", "core", "dom"))
    pairs, rows, width = amplitude.shape
    piece = rows // SPLITS
    holders = ny * nz * nc
    held = coupling_source.shape[0] // holders
    count = coupling_intersection.shape[0]
    capacity = nz * nc * 2

    with jax.named_scope("tables"):
        sources = coupling_source.reshape(ny, nz, nc, held)
        sources = lax.dynamic_index_in_dim(sources, z, 1, keepdims=False)
        sources = lax.dynamic_index_in_dim(sources, core, 1, keepdims=False)
        slots = lookup(pair_slot, sources)
        local = slots % pairs
        owner = slots // pairs
        mine = y * (nz * nc) + jnp.arange(nz * nc, dtype=jnp.int32)
        match = owner[:, None, :] == mine[None, :, None]
        low = jnp.min(jnp.where(match, local[:, None, :], pairs - 1), axis=2)
        high = jnp.max(jnp.where(match, local[:, None, :], 0), axis=2)
        picked = jnp.roll(jnp.stack([low, high], axis=2), -y, axis=0).reshape(ny, nz, nc, 2)
        z_numbers = jnp.arange(nz, dtype=jnp.int32)
        c_numbers = jnp.arange(nc, dtype=jnp.int32)
        ring_place = lookup(jnp.array(RING_PLACE, jnp.int32), (z_numbers - z) % nz)
        own_base = ((c_numbers != core) * (nz * pairs))[None, :] + (ring_place * pairs)[:, None]
        all_base = (z_numbers[:, None] * nc + c_numbers[None, :]) * pairs
        own_index = (picked + own_base[None, :, :, None]).reshape(-1)
        all_index = (picked + all_base[None, :, :, None]).reshape(-1)
        own_local = lax.dynamic_index_in_dim(local, y, 0, keepdims=False)
        own_owner = lax.dynamic_index_in_dim(owner, y, 0, keepdims=False)
        same = own_owner[:, None] == own_owner[None, :]
        least = jnp.min(jnp.where(same, own_local[None, :], pairs - 1), axis=1)
        second = (own_local > least).astype(jnp.int32)
        turned = (own_owner // (nz * nc) - y) % ny
        slot = turned * capacity + own_owner % (nz * nc) * 2 + second
        target = lax.dynamic_slice_in_dim(
            coupling_target, ((y * nz + z) * nc + core) * held + me * count, count, 0
        )
        target = lookup(pair_slot, target) % pairs

    def shift(array, step):
        return lax.ppermute(array, "y", [(i, (i + step) % ny) for i in range(ny)])

    stage_cost = pl.CostEstimate(flops=STAGE_FLOPS, bytes_accessed=STAGE_BYTES, transcendentals=0)
    landed = {}
    blocks = split(amplitude, piece)
    for (kind, members), block in zip(GROUPS, blocks):
        with jax.named_scope("along_z"):
            if kind == "ring":
                own = ring_gather(block)
                other = lax.ppermute(own, "core", [(i, 1 - i) for i in range(nc)])
                around, index = [own, other], own_index
            else:
                around, index = [lax.all_gather(block, ("z", "core"), axis=0)], all_index
        for n, member in enumerate(members):
            with jax.named_scope("along_y"):
                stay, ahead, far, back = pick(around, n, index, ny, "pick_y")
                from_back = shift(ahead, 1)
                from_ahead = shift(back, -1)
                from_far = shift(far, 2)
            with jax.named_scope("along_x"):
                here = [part[None, None] for part in (stay, from_ahead, from_far, from_back)]
                leaving = pick(here, 0, slot, 1, "pick_x", stage_cost)[0]
                arrived = lax.all_to_all(leaving, "dom", 0, 0, tiled=True)
            landed[member] = arrived.reshape(quarters, count, piece, COLUMNS)
    total = None
    for stage in STAGES:
        final = stage is STAGES[-1]
        couple = make_couple(stage, total is None, final, count, rows, width, pairs, quarters)
        args = [target, coupling_fock, coupling_intersection]
        args += [landed[j, r] for j in stage for r in range(SPLITS)]
        if total is not None:
            args.append(total)
        with jax.named_scope("couple"):
            total = couple(*args)
    with jax.named_scope("sum_x"):
        shares = lax.all_to_all(total, "dom", 0, 0, tiled=True)
    coupled = jnp.sum(shares.astype(jnp.float32), axis=0)
    energy_rows = lax.dynamic_slice_in_dim(virtual_energy, me * rows, rows, 1)
    denominator = energy_rows[:, :, None] + virtual_energy[:, None, :] + occupied_gap[:, None, None]
    current = amplitude.astype(jnp.float32)
    residual = integrals.astype(jnp.float32) + denominator * current - coupled
    return current - residual / denominator, residual


def solution(mesh):
    fine = Mesh(mesh.devices.reshape(4, 8, 2, 4), ("y", "z", "core", "dom"))
    chips = ("y", "z", "core")
    in_specs = (
        P(chips, "dom", None),
        P(chips, "dom", None),
        P(chips, None),
        P(chips),
        P(),
        P(),
        P(),
        P(chips + ("dom",)),
        P(chips + ("dom",), None, None),
    )
    out_specs = (P(chips, "dom", None), P(chips, "dom", None))
    return jax.shard_map(per_device, mesh=fine, in_specs=in_specs, out_specs=out_specs, check_vma=False)
```

```python
import jax
import jax.numpy as jnp
from jax import lax
from jax.experimental import pallas as pl
from jax.experimental.pallas import tpu as pltpu
from jax.sharding import Mesh, PartitionSpec as P

COLUMNS = 128
SPLITS = 2
GROUPS = (
    ("ring", ((0, 0),)),
    ("gather", ((0, 1), (1, 0), (1, 1), (2, 0), (2, 1))),
)
STAGES = ((0, 1), (2,))
UNROLL = 8
RING_PLACE = (0, 2, 4, 6, 7, 5, 3, 1)
STAGE_FLOPS = 12_000_000_000
STAGE_BYTES = 36_000_000


def lookup(table, indices):
    places = jnp.arange(table.shape[0], dtype=jnp.int32)
    return jnp.sum(jnp.where(indices[..., None] == places, table, 0), axis=-1)


def ring_gather(block):
    count = lax.axis_size("z")
    up = [(i, (i + 1) % count) for i in range(count)]
    down = [(i, (i - 1) % count) for i in range(count)]
    parts = [block]
    above = below = block
    for _ in range(count // 2 - 1):
        above = lax.ppermute(above, "z", up)
        below = lax.ppermute(below, "z", down)
        parts += [above, below]
    half = block.shape[1] // 2
    above = lax.ppermute(above[:, :half], "z", up)
    below = lax.ppermute(below[:, half:], "z", down)
    parts.append(jnp.concatenate([above, below], axis=1))
    return jnp.stack(parts)


def split(amplitude, piece, members):
    pairs, _, _ = amplitude.shape

    def kernel(in_ref, out_ref):
        for n, (j, r) in enumerate(members):
            rows = slice(r * piece, (r + 1) * piece)
            lanes = slice(j * COLUMNS, (j + 1) * COLUMNS)
            for p in range(pairs):
                out_ref[n, p] = in_ref[p, rows, lanes]

    return pl.pallas_call(
        kernel,
        out_shape=jax.ShapeDtypeStruct((len(members), pairs, piece, COLUMNS), amplitude.dtype),
        name="split",
    )(amplitude)


def pick(arrays, member, index, outputs, name, cost=None):
    piece, lanes = arrays[0].shape[-2:]
    count = index.shape[0] // outputs
    sizes = [array.shape[0] * array.shape[2] for array in arrays]

    def kernel(index_ref, *refs):
        in_refs = refs[: len(arrays)]
        out_refs = refs[len(arrays) : len(arrays) + outputs]
        held, sems = refs[-2:]
        copies = []
        start = 0
        for n, ref in enumerate(in_refs):
            for lead in range(arrays[n].shape[0]):
                size = arrays[n].shape[2]
                copy = pltpu.make_async_copy(
                    ref.at[lead, member], held.at[pl.ds(start, size)], sems.at[len(copies)]
                )
                copy.start()
                copies.append(copy)
                start += size
        for copy in copies:
            copy.wait()

        def body(i, carry):
            for n in range(outputs):
                out_refs[n][i] = held[index_ref[n * count + i]]
            return carry

        lax.fori_loop(0, count, body, 0, unroll=8)

    result = pl.pallas_call(
        kernel,
        in_specs=[pl.BlockSpec(memory_space=pltpu.SMEM)] + [pl.BlockSpec(memory_space=pltpu.HBM if array.shape[1] > 1 else pl.ANY) for array in arrays],
        out_specs=[pl.BlockSpec(memory_space=pltpu.VMEM)] * outputs,
        out_shape=[jax.ShapeDtypeStruct((count, piece, lanes), arrays[0].dtype)] * outputs,
        scratch_shapes=[
            pltpu.VMEM((sum(sizes), piece, lanes), arrays[0].dtype),
            pltpu.SemaphoreType.DMA((sum(array.shape[0] for array in arrays),)),
        ],
        compiler_params=pltpu.CompilerParams(vmem_limit_bytes=52 * 1024 * 1024),
        cost_estimate=cost,
        name=name,
    )(index, *arrays)
    return result


def make_couple(stage, first, final, count, rows, width, pairs, quarters):
    columns = len(stage) * COLUMNS
    begin = stage[0] * COLUMNS
    blocks = len(stage) * SPLITS
    piece = rows // SPLITS

    def kernel(target, fock, s_ref, *rest):
        rest = list(rest)
        amp_refs = [rest.pop(0) for _ in range(blocks)]
        base_ref = None if first else rest.pop(0)
        out_ref = rest.pop(0)
        acc = rest.pop(0) if final else out_ref
        step = pl.program_id(0)
        fill = None if first else pltpu.make_async_copy(base_ref, acc, rest.pop(0))

        @pl.when(step == 0)
        def _():
            if first:
                for p in range(pairs):
                    acc[p] = jnp.zeros((width, width), jnp.float32)
            else:
                fill.start()

        lefts = []
        for g in range(UNROLL):
            strips = []
            for b in range(0, blocks, SPLITS):
                pieces = [amp_refs[b + r][q, g] for q in range(quarters) for r in range(SPLITS)]
                strips.append(jnp.concatenate(pieces, axis=0))
            amp = strips[0] if len(strips) == 1 else jnp.concatenate(strips, axis=1)
            left = jnp.dot(s_ref[g], amp, preferred_element_type=jnp.float32)
            lefts.append(left.astype(jnp.bfloat16))
        if not first:

            @pl.when(step == 0)
            def _():
                fill.wait()

        for g in range(UNROLL):
            part = lax.dot_general(
                lefts[g],
                s_ref[g, :, begin : begin + columns],
                (((1,), (1,)), ((), ())),
                preferred_element_type=jnp.float32,
            )
            c = step * UNROLL + g
            acc[target[c]] += fock[c] * part
        if final:

            @pl.when(step == count // UNROLL - 1)
            def _():
                for p in range(pairs):
                    for q in range(quarters):
                        out_ref[q, p] = acc[p, q * rows : (q + 1) * rows, :].astype(jnp.bfloat16)

    whole = pl.BlockSpec((pairs, width, width), lambda i, *_: (0, 0, 0), pipeline_mode=pl.Buffered(1))
    in_specs = [pl.BlockSpec((UNROLL, width, width), lambda i, *_: (i, 0, 0))]
    in_specs += [pl.BlockSpec((quarters, UNROLL, piece, COLUMNS), lambda i, *_: (0, i, 0, 0))] * blocks
    if not first:
        in_specs.append(pl.BlockSpec(memory_space=pl.ANY))
    scratch = []
    if final:
        out_shape = jax.ShapeDtypeStruct((quarters, pairs, rows, width), jnp.bfloat16)
        out_specs = pl.BlockSpec((quarters, pairs, rows, width), lambda i, *_: (0, 0, 0, 0))
        scratch.append(pltpu.VMEM((pairs, width, width), jnp.float32))
        if not first:
            scratch.append(pltpu.SemaphoreType.DMA)
    else:
        out_shape = jax.ShapeDtypeStruct((pairs, width, width), jnp.float32)
        out_specs = whole
    return pl.pallas_call(
        kernel,
        grid_spec=pltpu.PrefetchScalarGridSpec(
            num_scalar_prefetch=2,
            grid=(count // UNROLL,),
            in_specs=in_specs,
            out_specs=out_specs,
            scratch_shapes=scratch,
        ),
        out_shape=out_shape,
        compiler_params=pltpu.CompilerParams(vmem_limit_bytes=52 * 1024 * 1024),
        cost_estimate=pl.CostEstimate(
            flops=8 * count * width * width * columns,
            bytes_accessed=count * width * width * 3,
            transcendentals=0,
        ),
        name="couple",
    )


def per_device(
    amplitude,
    integrals,
    virtual_energy,
    occupied_gap,
    pair_slot,
    coupling_source,
    coupling_target,
    coupling_fock,
    coupling_intersection,
):
    ny, nz, nc, quarters = (lax.axis_size(a) for a in ("y", "z", "core", "dom"))
    y, z, core, me = (lax.axis_index(a) for a in ("y", "z", "core", "dom"))
    pairs, rows, width = amplitude.shape
    piece = rows // SPLITS
    holders = ny * nz * nc
    held = coupling_source.shape[0] // holders
    count = coupling_intersection.shape[0]
    capacity = nz * nc * 2

    with jax.named_scope("tables"):
        sources = coupling_source.reshape(ny, nz, nc, held)
        sources = lax.dynamic_index_in_dim(sources, z, 1, keepdims=False)
        sources = lax.dynamic_index_in_dim(sources, core, 1, keepdims=False)
        slots = lookup(pair_slot, sources)
        local = slots % pairs
        owner = slots // pairs
        mine = y * (nz * nc) + jnp.arange(nz * nc, dtype=jnp.int32)
        match = owner[:, None, :] == mine[None, :, None]
        low = jnp.min(jnp.where(match, local[:, None, :], pairs - 1), axis=2)
        high = jnp.max(jnp.where(match, local[:, None, :], 0), axis=2)
        picked = jnp.roll(jnp.stack([low, high], axis=2), -y, axis=0).reshape(ny, nz, nc, 2)
        z_numbers = jnp.arange(nz, dtype=jnp.int32)
        c_numbers = jnp.arange(nc, dtype=jnp.int32)
        ring_place = lookup(jnp.array(RING_PLACE, jnp.int32), (z_numbers - z) % nz)
        own_base = ((c_numbers != core) * (nz * pairs))[None, :] + (ring_place * pairs)[:, None]
        all_base = (z_numbers[:, None] * nc + c_numbers[None, :]) * pairs
        own_index = (picked + own_base[None, :, :, None]).reshape(-1)
        all_index = (picked + all_base[None, :, :, None]).reshape(-1)
        own_local = lax.dynamic_index_in_dim(local, y, 0, keepdims=False)
        own_owner = lax.dynamic_index_in_dim(owner, y, 0, keepdims=False)
        same = own_owner[:, None] == own_owner[None, :]
        least = jnp.min(jnp.where(same, own_local[None, :], pairs - 1), axis=1)
        second = (own_local > least).astype(jnp.int32)
        turned = (own_owner // (nz * nc) - y) % ny
        slot = turned * capacity + own_owner % (nz * nc) * 2 + second
        target = lax.dynamic_slice_in_dim(
            coupling_target, ((y * nz + z) * nc + core) * held + me * count, count, 0
        )
        target = lookup(pair_slot, target) % pairs

    def shift(array, step):
        return lax.ppermute(array, "y", [(i, (i + step) % ny) for i in range(ny)])

    stage_cost = pl.CostEstimate(flops=STAGE_FLOPS, bytes_accessed=STAGE_BYTES, transcendentals=0)
    landed = {}
    for kind, members in GROUPS:
        block = split(amplitude, piece, members)
        with jax.named_scope("along_z"):
            if kind == "ring":
                own = ring_gather(block)
                other = lax.ppermute(own, "core", [(i, 1 - i) for i in range(nc)])
                around, index = [own, other], own_index
            else:
                around, index = [lax.all_gather(block, ("z", "core"), axis=0)], all_index
        for n, member in enumerate(members):
            with jax.named_scope("along_y"):
                stay, ahead, far, back = pick(around, n, index, ny, "pick_y")
                from_back = shift(ahead, 1)
                from_ahead = shift(back, -1)
                from_far = shift(far, 2)
            with jax.named_scope("along_x"):
                here = [part[None, None] for part in (stay, from_ahead, from_far, from_back)]
                leaving = pick(here, 0, slot, 1, "pick_x", stage_cost)[0]
                arrived = lax.all_to_all(leaving, "dom", 0, 0, tiled=True)
            landed[member] = arrived.reshape(quarters, count, piece, COLUMNS)
    total = None
    for stage in STAGES:
        final = stage is STAGES[-1]
        couple = make_couple(stage, total is None, final, count, rows, width, pairs, quarters)
        args = [target, coupling_fock, coupling_intersection]
        args += [landed[j, r] for j in stage for r in range(SPLITS)]
        if total is not None:
            args.append(total)
        with jax.named_scope("couple"):
            total = couple(*args)
    with jax.named_scope("sum_x"):
        shares = lax.all_to_all(total, "dom", 0, 0, tiled=True)
    coupled = jnp.sum(shares.astype(jnp.float32), axis=0)
    energy_rows = lax.dynamic_slice_in_dim(virtual_energy, me * rows, rows, 1)
    denominator = energy_rows[:, :, None] + virtual_energy[:, None, :] + occupied_gap[:, None, None]
    current = amplitude.astype(jnp.float32)
    residual = integrals.astype(jnp.float32) + denominator * current - coupled
    return current - residual / denominator, residual


def solution(mesh):
    fine = Mesh(mesh.devices.reshape(4, 8, 2, 4), ("y", "z", "core", "dom"))
    chips = ("y", "z", "core")
    in_specs = (
        P(chips, "dom", None),
        P(chips, "dom", None),
        P(chips, None),
        P(chips),
        P(),
        P(),
        P(),
        P(chips + ("dom",)),
        P(chips + ("dom",), None, None),
    )
    out_specs = (P(chips, "dom", None), P(chips, "dom", None))
    return jax.shard_map(per_device, mesh=fine, in_specs=in_specs, out_specs=out_specs, check_vma=False)
```

```python
import jax
import jax.numpy as jnp
from jax import lax
from jax.experimental import pallas as pl
from jax.experimental.pallas import tpu as pltpu
from jax.sharding import Mesh, PartitionSpec as P

COLUMNS = 128
SPLITS = 2
GROUPS = (
    ("ring", ((0, 0),)),
    ("gather", ((0, 1), (1, 0), (1, 1), (2, 0), (2, 1))),
)
STAGES = ((0, 1), (2,))
UNROLL = 8
RING_PLACE = (0, 2, 4, 6, 7, 5, 3, 1)
STAGE_FLOPS = 12_000_000_000
STAGE_BYTES = 36_000_000


def lookup(table, indices):
    places = jnp.arange(table.shape[0], dtype=jnp.int32)
    return jnp.sum(jnp.where(indices[..., None] == places, table, 0), axis=-1)


def ring_gather(block):
    count = lax.axis_size("z")

    def shift(array, step):
        return lax.ppermute(array, "z", [(i, (i + step) % count) for i in range(count)])

    one_above, one_below = shift(block, 1), shift(block, -1)
    two_above, two_below = shift(block, 2), shift(block, -2)
    three_above, three_below = shift(two_above, 1), shift(two_below, -1)
    half = block.shape[1] // 2
    across = [shift(two_above[:, :half], 2), shift(two_below[:, half:], -2)]
    parts = [block, one_above, one_below, two_above, two_below, three_above, three_below]
    return jnp.stack(parts + [jnp.concatenate(across, axis=1)])


def split(amplitude, piece, members):
    pairs, _, _ = amplitude.shape

    if len(members) == 1:
        j, r = members[0]
        return pl.pallas_call(
            lambda in_ref, out_ref: out_ref.__setitem__(0, in_ref[...]),
            grid=(1,),
            in_specs=[pl.BlockSpec((pairs, piece, COLUMNS), lambda i: (0, r, j))],
            out_specs=pl.BlockSpec((1, pairs, piece, COLUMNS), lambda i: (0, 0, 0, 0)),
            out_shape=jax.ShapeDtypeStruct((1, pairs, piece, COLUMNS), amplitude.dtype),
            name="first_piece",
        )(amplitude)

    def kernel(in_ref, out_ref):
        for n, (j, r) in enumerate(members):
            rows = slice(r * piece, (r + 1) * piece)
            lanes = slice(j * COLUMNS, (j + 1) * COLUMNS)
            for p in range(pairs):
                out_ref[n, p] = in_ref[p, rows, lanes]

    return pl.pallas_call(
        kernel,
        out_shape=jax.ShapeDtypeStruct((len(members), pairs, piece, COLUMNS), amplitude.dtype),
        name="split",
    )(amplitude)


def pick(arrays, member, index, outputs, name, cost=None):
    piece, lanes = arrays[0].shape[-2:]
    count = index.shape[0] // outputs
    sizes = [array.shape[0] * array.shape[2] for array in arrays]

    def kernel(index_ref, *refs):
        in_refs = refs[: len(arrays)]
        out_refs = refs[len(arrays) : len(arrays) + outputs]
        held, sems = refs[-2:]
        copies = []
        start = 0
        for n, ref in enumerate(in_refs):
            for lead in range(arrays[n].shape[0]):
                size = arrays[n].shape[2]
                copy = pltpu.make_async_copy(
                    ref.at[lead, member], held.at[pl.ds(start, size)], sems.at[len(copies)]
                )
                copy.start()
                copies.append(copy)
                start += size
        for copy in copies:
            copy.wait()

        def body(i, carry):
            for n in range(outputs):
                out_refs[n][i] = held[index_ref[n * count + i]]
            return carry

        lax.fori_loop(0, count, body, 0, unroll=8)

    result = pl.pallas_call(
        kernel,
        in_specs=[pl.BlockSpec(memory_space=pltpu.SMEM)] + [pl.BlockSpec(memory_space=pltpu.HBM if array.shape[1] > 1 else pl.ANY) for array in arrays],
        out_specs=[pl.BlockSpec(memory_space=pltpu.VMEM)] * outputs,
        out_shape=[jax.ShapeDtypeStruct((count, piece, lanes), arrays[0].dtype)] * outputs,
        scratch_shapes=[
            pltpu.VMEM((sum(sizes), piece, lanes), arrays[0].dtype),
            pltpu.SemaphoreType.DMA((sum(array.shape[0] for array in arrays),)),
        ],
        compiler_params=pltpu.CompilerParams(vmem_limit_bytes=52 * 1024 * 1024),
        cost_estimate=cost,
        name=name,
    )(index, *arrays)
    return result


def make_couple(stage, first, final, count, rows, width, pairs, quarters):
    columns = len(stage) * COLUMNS
    begin = stage[0] * COLUMNS
    blocks = len(stage) * SPLITS
    piece = rows // SPLITS

    def kernel(target, fock, s_ref, *rest):
        rest = list(rest)
        amp_refs = [rest.pop(0) for _ in range(blocks)]
        base_ref = None if first else rest.pop(0)
        out_ref = rest.pop(0)
        acc = rest.pop(0) if final else out_ref
        step = pl.program_id(0)
        fill = None if first else pltpu.make_async_copy(base_ref, acc, rest.pop(0))

        @pl.when(step == 0)
        def _():
            if first:
                for p in range(pairs):
                    acc[p] = jnp.zeros((width, width), jnp.float32)
            else:
                fill.start()

        lefts = []
        for g in range(UNROLL):
            strips = []
            for b in range(0, blocks, SPLITS):
                pieces = [amp_refs[b + r][q, g] for q in range(quarters) for r in range(SPLITS)]
                strips.append(jnp.concatenate(pieces, axis=0))
            amp = strips[0] if len(strips) == 1 else jnp.concatenate(strips, axis=1)
            left = jnp.dot(s_ref[g], amp, preferred_element_type=jnp.float32)
            lefts.append(left.astype(jnp.bfloat16))
        if not first:

            @pl.when(step == 0)
            def _():
                fill.wait()

        for g in range(UNROLL):
            part = lax.dot_general(
                lefts[g],
                s_ref[g, :, begin : begin + columns],
                (((1,), (1,)), ((), ())),
                preferred_element_type=jnp.float32,
            )
            c = step * UNROLL + g
            acc[target[c]] += fock[c] * part
        if final:

            @pl.when(step == count // UNROLL - 1)
            def _():
                for p in range(pairs):
                    for q in range(quarters):
                        out_ref[q, p] = acc[p, q * rows : (q + 1) * rows, :].astype(jnp.bfloat16)

    whole = pl.BlockSpec((pairs, width, width), lambda i, *_: (0, 0, 0), pipeline_mode=pl.Buffered(1))
    in_specs = [pl.BlockSpec((UNROLL, width, width), lambda i, *_: (i, 0, 0))]
    in_specs += [pl.BlockSpec((quarters, UNROLL, piece, COLUMNS), lambda i, *_: (0, i, 0, 0))] * blocks
    if not first:
        in_specs.append(pl.BlockSpec(memory_space=pl.ANY))
    scratch = []
    if final:
        out_shape = jax.ShapeDtypeStruct((quarters, pairs, rows, width), jnp.bfloat16)
        out_specs = pl.BlockSpec((quarters, pairs, rows, width), lambda i, *_: (0, 0, 0, 0))
        scratch.append(pltpu.VMEM((pairs, width, width), jnp.float32))
        if not first:
            scratch.append(pltpu.SemaphoreType.DMA)
    else:
        out_shape = jax.ShapeDtypeStruct((pairs, width, width), jnp.float32)
        out_specs = whole
    return pl.pallas_call(
        kernel,
        grid_spec=pltpu.PrefetchScalarGridSpec(
            num_scalar_prefetch=2,
            grid=(count // UNROLL,),
            in_specs=in_specs,
            out_specs=out_specs,
            scratch_shapes=scratch,
        ),
        out_shape=out_shape,
        compiler_params=pltpu.CompilerParams(vmem_limit_bytes=52 * 1024 * 1024),
        cost_estimate=pl.CostEstimate(
            flops=8 * count * width * width * columns,
            bytes_accessed=count * width * width * 3,
            transcendentals=0,
        ),
        name="couple",
    )


def per_device(
    amplitude,
    integrals,
    virtual_energy,
    occupied_gap,
    pair_slot,
    coupling_source,
    coupling_target,
    coupling_fock,
    coupling_intersection,
):
    ny, nz, nc, quarters = (lax.axis_size(a) for a in ("y", "z", "core", "dom"))
    y, z, core, me = (lax.axis_index(a) for a in ("y", "z", "core", "dom"))
    pairs, rows, width = amplitude.shape
    piece = rows // SPLITS
    holders = ny * nz * nc
    held = coupling_source.shape[0] // holders
    count = coupling_intersection.shape[0]
    capacity = nz * nc * 2

    with jax.named_scope("tables"):
        sources = coupling_source.reshape(ny, nz, nc, held)
        sources = lax.dynamic_index_in_dim(sources, z, 1, keepdims=False)
        sources = lax.dynamic_index_in_dim(sources, core, 1, keepdims=False)
        slots = lookup(pair_slot, sources)
        local = slots % pairs
        owner = slots // pairs
        mine = y * (nz * nc) + jnp.arange(nz * nc, dtype=jnp.int32)
        match = owner[:, None, :] == mine[None, :, None]
        low = jnp.min(jnp.where(match, local[:, None, :], pairs - 1), axis=2)
        high = jnp.max(jnp.where(match, local[:, None, :], 0), axis=2)
        picked = jnp.roll(jnp.stack([low, high], axis=2), -y, axis=0).reshape(ny, nz, nc, 2)
        z_numbers = jnp.arange(nz, dtype=jnp.int32)
        c_numbers = jnp.arange(nc, dtype=jnp.int32)
        ring_place = lookup(jnp.array(RING_PLACE, jnp.int32), (z_numbers - z) % nz)
        own_base = ((c_numbers != core) * (nz * pairs))[None, :] + (ring_place * pairs)[:, None]
        all_base = (z_numbers[:, None] * nc + c_numbers[None, :]) * pairs
        own_index = (picked + own_base[None, :, :, None]).reshape(-1)
        all_index = (picked + all_base[None, :, :, None]).reshape(-1)
        own_local = lax.dynamic_index_in_dim(local, y, 0, keepdims=False)
        own_owner = lax.dynamic_index_in_dim(owner, y, 0, keepdims=False)
        same = own_owner[:, None] == own_owner[None, :]
        least = jnp.min(jnp.where(same, own_local[None, :], pairs - 1), axis=1)
        second = (own_local > least).astype(jnp.int32)
        turned = (own_owner // (nz * nc) - y) % ny
        slot = turned * capacity + own_owner % (nz * nc) * 2 + second
        target = lax.dynamic_slice_in_dim(
            coupling_target, ((y * nz + z) * nc + core) * held + me * count, count, 0
        )
        target = lookup(pair_slot, target) % pairs

    def shift(array, step):
        return lax.ppermute(array, "y", [(i, (i + step) % ny) for i in range(ny)])

    stage_cost = pl.CostEstimate(flops=STAGE_FLOPS, bytes_accessed=STAGE_BYTES, transcendentals=0)
    landed = {}
    for kind, members in GROUPS:
        block = split(amplitude, piece, members)
        with jax.named_scope("along_z"):
            if kind == "ring":
                own = ring_gather(block)
                other = lax.ppermute(own, "core", [(i, 1 - i) for i in range(nc)])
                around, index = [own, other], own_index
            else:
                everyone = lax.all_gather(block, ("z", "core"), axis=0)
                everyone, _ = lax.optimization_barrier((everyone, leaving))
                around, index = [everyone], all_index
        for n, member in enumerate(members):
            with jax.named_scope("along_y"):
                stay, ahead, far, back = pick(around, n, index, ny, "pick_y")
                from_back = shift(ahead, 1)
                from_ahead = shift(back, -1)
                from_far = shift(far, 2)
            with jax.named_scope("along_x"):
                here = [part[None, None] for part in (stay, from_ahead, from_far, from_back)]
                leaving = pick(here, 0, slot, 1, "pick_x", stage_cost)[0]
                arrived = lax.all_to_all(leaving, "dom", 0, 0, tiled=True)
            landed[member] = arrived.reshape(quarters, count, piece, COLUMNS)
    total = None
    for stage in STAGES:
        final = stage is STAGES[-1]
        couple = make_couple(stage, total is None, final, count, rows, width, pairs, quarters)
        args = [target, coupling_fock, coupling_intersection]
        args += [landed[j, r] for j in stage for r in range(SPLITS)]
        if total is not None:
            args.append(total)
        with jax.named_scope("couple"):
            total = couple(*args)
    with jax.named_scope("sum_x"):
        shares = lax.all_to_all(total, "dom", 0, 0, tiled=True)
    coupled = jnp.sum(shares.astype(jnp.float32), axis=0)
    energy_rows = lax.dynamic_slice_in_dim(virtual_energy, me * rows, rows, 1)
    denominator = energy_rows[:, :, None] + virtual_energy[:, None, :] + occupied_gap[:, None, None]
    current = amplitude.astype(jnp.float32)
    residual = integrals.astype(jnp.float32) + denominator * current - coupled
    return current - residual / denominator, residual


def solution(mesh):
    fine = Mesh(mesh.devices.reshape(4, 8, 2, 4), ("y", "z", "core", "dom"))
    chips = ("y", "z", "core")
    in_specs = (
        P(chips, "dom", None),
        P(chips, "dom", None),
        P(chips, None),
        P(chips),
        P(),
        P(),
        P(),
        P(chips + ("dom",)),
        P(chips + ("dom",), None, None),
    )
    out_specs = (P(chips, "dom", None), P(chips, "dom", None))
    return jax.shard_map(per_device, mesh=fine, in_specs=in_specs, out_specs=out_specs, check_vma=False)
```
